32 devices in a mesh: groups: 2 (over y), store: 4 (over x, core), tp: 4 (over z).
Axes of the slice: x: 2, y: 2, z: 4, core: 2. Of those that a mesh axis runs over, the one named last changes fastest.
Arguments:
- pool: bfloat16 [1, 128, 128, 8, 2, 128], P(None, ('groups', 'store'), 'tp'), parts along dimension 1, may hold values from -6 to 6
- table: int32 [8, 1, 16], P('groups'), parts along dimension 0, may hold values from 0 to 63, as said below
- hist_len: int32 [8], P('groups'), parts along dimension 0, may hold values from 1 to 1024, as said below
- new_len: int32 [8], P('groups'), parts along dimension 0, may hold values from 2 to 1024, as said below
- queries: bfloat16 [1, 8, 1024, 96, 128], P(None, ('groups', 'store'), None, 'tp'), parts along dimension 1, may hold values from -16 to 16
- new_kv: bfloat16 [1, 8, 1024, 8, 2, 128], P(None, ('groups', 'store'), None, 'tp'), parts along dimension 1, may hold values from -16 to 16
Outputs:
- attended: bfloat16 [1, 8, 1024, 96, 128], P(None, ('groups', 'store'), None, 'tp'), parts along dimension 1
- new_pool: bfloat16 [1, 128, 128, 8, 2, 128], P(None, ('groups', 'store'), 'tp'), parts along dimension 1
The draws below stay inside these ranges and needn't reach their ends.
There are 2 independent parts, one for each index of `groups`. The reference program is written for one: setup_inputs(seed, part) draws one part's arguments, and reference() takes and returns one part's arrays. A program takes and returns all parts, laid end to end along the dimension named above; each array names one. Nothing has to cross between parts.
Inputs may be any that keep to these rules, and one draw needn't show every extreme that they name: For each layer, table maps the 4 x 16 pairs (session, block) one to one onto the slots; slot g lies on store index g // 16. Blocks 0 to 7 hold history, the others receive the new turn. Each store index holds exactly 4 blocks of each session in each layer, and at most 4 new-turn blocks of one session in one layer, a bound that some session reaches in every layer; where 4 is 1 this means that a session's 8 new-turn blocks lie on 8 distinct store indices. `hist_len`: some session has all 1024 tokens. `new_len`: some session has all 1024 tokens.
All inputs are finite; a program needn't handle non-finite values.
Results may differ from the reference program's by a relative error of at most 0.0045.
Values may be sent and summed in bfloat16 or wider, within the bound.
A program may use at most 128 MiB of HBM per device.

```python
import math
import jax
import jax.numpy as jnp
from jax import lax

HEADS = 96
KVH = 8
HD = 128
LAYERS = 1
BLOCK = 128
HB = 16
NEW = 1024
SESS = 4
NB = 8
HIST_BLK = 8
HIST = 1024
SLOTS = 64


def draw_queries(key, part):
    key = jax.random.fold_in(key, 11)
    shape = (LAYERS, SESS, NEW, HEADS, HD)
    values = jax.random.truncated_normal(key, -6.0, 6.0, shape, jnp.float32)
    return values.astype(jnp.bfloat16)


def draw_new_kv(key, part):
    key = jax.random.fold_in(key, 13)
    shape = (LAYERS, SESS, NEW, KVH, 2, HD)
    values = jax.random.truncated_normal(key, -6.0, 6.0, shape, jnp.float32)
    return values.astype(jnp.bfloat16)


def permute_rows(key_list, length):
    return jax.vmap(lambda single_key: jax.random.permutation(single_key, length))(key_list)


def draw_table(key, part):
    key = jax.random.fold_in(key, 5)
    per_store = HB // SESS
    key_list = jax.random.split(key, 3)
    positions = permute_rows(jax.random.split(key_list[0], LAYERS * SESS), HB).reshape(LAYERS, SESS, HB)
    forced = jax.random.randint(key_list[1], (LAYERS,), 0, SESS)
    rotated = (jnp.arange(HB) + NB) % HB
    pick_rows = (jnp.arange(SESS)[None, :] == forced[:, None])[:, :, None]
    positions = jnp.where(pick_rows, rotated[None, None, :], positions)
    local_slots = permute_rows(jax.random.split(key_list[2], LAYERS * SESS), HB).reshape(LAYERS, SESS, HB)
    device = positions // per_store
    within = positions % per_store
    paired = jnp.arange(SESS)[None, :, None] * per_store + within
    gathered = local_slots[jnp.arange(LAYERS)[:, None, None], device, paired]
    slots = device * HB + gathered
    return jnp.transpose(slots, (1, 0, 2)).astype(jnp.int32)


def lengths_with_top(key, lowest, highest):
    draw_key, pick_key = jax.random.split(key)
    counts = jax.random.randint(draw_key, (SESS,), lowest, highest + 1)
    chosen = jax.random.randint(pick_key, (), 0, SESS)
    return jnp.where(jnp.arange(SESS) == chosen, highest, counts).astype(jnp.int32)


def draw_hist_len(key, part):
    key = jax.random.fold_in(key, 7)
    return lengths_with_top(key, 1, HIST)


def draw_new_len(key, part):
    key = jax.random.fold_in(key, 9)
    return lengths_with_top(key, 2, NEW)


def levels(own_key, extent, cuts, least, top_value):
    gain, own = 1.0, jax.random.fold_in(own_key, 6)
    for dim, parts in cuts:
        draws = jnp.exp(jax.random.uniform(jax.random.fold_in(own, dim), (parts,), jnp.float32, least / len(cuts), top_value / len(cuts)))
        gain = gain * jnp.repeat(draws, extent[dim] // parts).reshape([-1 if axis == dim else 1 for axis in range(len(extent))])
    return gain


def centred(stream_key, shape, width, most, cuts=(), kind=jnp.bfloat16):
    values = jax.random.normal(stream_key, shape, jnp.float32) * width
    if len(cuts) > 0:
        values = levels(stream_key, shape, cuts, -0.22, 0.18) * values
    return jnp.clip(values, min=-most, max=most).astype(kind)


def setup_inputs(seed: int = 0, part: int = 0) -> dict:
    key_of = jax.random.split(jax.random.key(seed), 7)
    part_splits = jax.random.split(jax.random.fold_in(key_of[6], part), 7)
    pool = centred(part_splits[0], (LAYERS, SLOTS, BLOCK, KVH, 2, HD), 1.0, 6.0, ((1, 4), (2, 4)))
    table = draw_table(jax.random.fold_in(jax.random.fold_in(key_of[6], part), 71), part)
    hist_len = draw_hist_len(jax.random.fold_in(jax.random.fold_in(key_of[6], part), 71), part)
    new_len = draw_new_len(jax.random.fold_in(jax.random.fold_in(key_of[6], part), 71), part)
    queries = draw_queries(jax.random.fold_in(jax.random.fold_in(key_of[6], part), 71), part)
    new_kv = draw_new_kv(jax.random.fold_in(jax.random.fold_in(key_of[6], part), 71), part)
    return dict(pool=pool, table=table, hist_len=hist_len, new_len=new_len, queries=queries, new_kv=new_kv)


def attend_pair(query, history, fresh, hist_count, new_count):
    keys_all = jnp.concatenate([history, fresh], axis=0).astype(jnp.float32)
    group_size = HEADS // KVH
    grouped = query.astype(jnp.float32).reshape(NEW, KVH, group_size, HD)
    scores = jnp.einsum('qkgd,tkd->kgqt', grouped, keys_all[:, :, 0, :]) * (1.0 / math.sqrt(HD))
    token_ids = jnp.arange(HIST + NEW).astype(jnp.int32)
    row_ids = jnp.arange(NEW).astype(jnp.int32)
    valid = jnp.where(token_ids[None, :] < HIST, token_ids[None, :] < hist_count, token_ids[None, :] - HIST <= row_ids[:, None])
    masked = jnp.where(valid, scores, -jnp.inf)
    row_peak = lax.optimization_barrier(jnp.max(masked, axis=-1, keepdims=True))
    weights = jnp.where(valid, jnp.exp(masked - row_peak), 0.0)
    weight_sum = lax.optimization_barrier(jnp.sum(weights, axis=-1))
    probs = lax.optimization_barrier(weights.astype(jnp.bfloat16)).astype(jnp.float32)
    blended = jnp.einsum('kgqt,tkd->qkgd', probs, keys_all[:, :, 1, :])
    blended = blended / jnp.transpose(weight_sum, (2, 0, 1))[..., None]
    blended = jnp.where((row_ids < new_count)[:, None, None, None], blended, 0.0)
    return blended.reshape(NEW, HEADS, HD).astype(jnp.bfloat16)

def reference(pool, table, hist_len, new_len, queries, new_kv):
    token_ids = jnp.arange(NEW).astype(jnp.int32)
    keep = token_ids[None, None, :] < new_len[None, :, None]
    fresh_all = jnp.where(keep[:, :, :, None, None, None], new_kv, jnp.zeros_like(new_kv))

    def attend_index(flat_index):
        layer_index = flat_index // SESS
        session = flat_index % SESS
        slot_ids = table[session, layer_index, :HIST_BLK].astype(jnp.int32)
        history = pool[layer_index][slot_ids].reshape(HIST, KVH, 2, HD)
        return attend_pair(queries[layer_index, session], history, fresh_all[layer_index, session], hist_len[session], new_len[session])
    attended = lax.map(attend_index, jnp.arange(LAYERS * SESS).astype(jnp.int32))
    attended = attended.reshape(LAYERS, SESS, NEW, HEADS, HD)
    fresh_blocks = fresh_all.reshape(LAYERS, SESS * NB, BLOCK, KVH, 2, HD)
    new_pool = pool
    for layer_index in range(LAYERS):
        targets = table[:, layer_index, HIST_BLK:].reshape(-1).astype(jnp.int32)
        new_pool = new_pool.at[layer_index, targets].set(fresh_blocks[layer_index])
    return (attended, new_pool)
```

```python
import functools
import math

import jax
import jax.numpy as jnp
from jax import lax
from jax.experimental import pallas as pl
from jax.experimental.pallas import tpu as pltpu
from jax.sharding import PartitionSpec as P

NT = (((1,), (1,)), ((), ()))
VMEM_BYTES = 48 * 1024 * 1024


def scaled_pair(q, factor):
    full = q.astype(jnp.float32) * factor
    high = full.astype(jnp.bfloat16)
    low = (full - high.astype(jnp.float32)).astype(jnp.bfloat16)
    return jnp.concatenate([high, low], axis=1)


def scores_of(q2, keys):
    return lax.dot_general(q2, keys, NT, preferred_element_type=jnp.float32)


def split_kv(kv, kd, vd, rows):
    hd = kv.shape[1] // 2
    kd[rows, :hd] = kv[:, :hd]
    kd[rows, hd:] = kv[:, :hd]
    vd[rows, :hd] = kv[:, hd:]
    vd[rows, hd:] = jnp.ones((kv.shape[0], hd), kv.dtype)


def head_loop(group, unroll, body):
    def step(n, carry):
        for u in range(unroll):
            body(n * unroll + u)
        return carry

    lax.fori_loop(0, group // unroll, step, 0)


def fresh_kernel(group, hd, factor, new_ref, q_ref, kv_ref, o_ref, lse_ref, kd, vd):
    i = pl.program_id(1)
    bq = q_ref.shape[0]
    steps = kd.shape[0] // bq

    @pl.when(i == 0)
    def _():
        split_kv(kv_ref[...], kd, vd, slice(None))

    def variant(n):
        lanes = lax.broadcasted_iota(jnp.int32, (bq, 128), 1)
        causal = lax.broadcasted_iota(jnp.int32, (bq, bq), 1) <= lax.broadcasted_iota(
            jnp.int32, (bq, bq), 0
        )

        def head(g):
            cols = pl.ds(pl.multiple_of(g * hd, hd), hd)
            q2 = scaled_pair(q_ref[:, cols], factor)
            edge = jnp.where(causal, scores_of(q2, kd[n * bq : (n + 1) * bq, :]), -jnp.inf)
            peak = jnp.max(edge, axis=1, keepdims=True)
            if n > 0:
                full = scores_of(q2, kd[: n * bq, :])
                peak = jnp.maximum(peak, jnp.max(full, axis=1, keepdims=True))
            p = jnp.exp2(edge - peak).astype(jnp.bfloat16)
            acc = jnp.dot(
                p, vd[n * bq : (n + 1) * bq, :], preferred_element_type=jnp.float32
            )
            if n > 0:
                p = jnp.exp2(full - peak).astype(jnp.bfloat16)
                acc += jnp.dot(p, vd[: n * bq, :], preferred_element_type=jnp.float32)
            total = acc[:, hd:]
            o_ref[:, cols] = acc[:, :hd] / total
            lse_ref[0] = jnp.where(lanes == g, peak + jnp.log2(total), lse_ref[0])

        head_loop(group, 2, head)

    for n in range(steps):
        pl.when((i == n) & (i * bq < new_ref[0]))(functools.partial(variant, n))


def hist_kernel(group, hd, factor, lens_ref, q_ref, kv_ref, of_ref, lse_ref, o_ref, kd, vd):
    i = pl.program_id(1)
    bq = q_ref.shape[0]
    chunk = min(256, kd.shape[0])
    chunks = kd.shape[0] // chunk
    hist_count = lens_ref[0]
    new_count = lens_ref[1]

    @pl.when(i == 0)
    def _():
        tp, blocks, piece, _ = kv_ref.shape
        for b in range(blocks):
            for z in range(tp):
                begin = (b * tp + z) * piece
                split_kv(kv_ref[z, b], kd, vd, slice(begin, begin + piece))

    def variant(n):
        lanes = lax.broadcasted_iota(jnp.int32, (bq, 128), 1)
        valid = lax.broadcasted_iota(jnp.int32, (bq, chunk), 1) < hist_count - n * chunk
        keep = lax.broadcasted_iota(jnp.int32, (bq, hd), 0) < new_count - i * bq

        def head(g):
            cols = pl.ds(pl.multiple_of(g * hd, hd), hd)
            q2 = scaled_pair(q_ref[:, cols], factor)
            lse = jnp.sum(jnp.where(lanes == g, lse_ref[0], 0.0), axis=1, keepdims=True)
            edge = jnp.where(valid, scores_of(q2, kd[n * chunk : (n + 1) * chunk, :]), -jnp.inf)
            peak = jnp.maximum(lse, jnp.max(edge, axis=1, keepdims=True))
            if n > 0:
                full = scores_of(q2, kd[: n * chunk, :])
                peak = jnp.maximum(peak, jnp.max(full, axis=1, keepdims=True))
            p = jnp.exp2(edge - peak).astype(jnp.bfloat16)
            acc = jnp.dot(
                p, vd[n * chunk : (n + 1) * chunk, :], preferred_element_type=jnp.float32
            )
            if n > 0:
                p = jnp.exp2(full - peak).astype(jnp.bfloat16)
                acc += jnp.dot(p, vd[: n * chunk, :], preferred_element_type=jnp.float32)
            share = jnp.exp2(lse - peak)
            out = (acc[:, :hd] + share * of_ref[:, cols]) / (acc[:, hd:] + share)
            o_ref[:, cols] = jnp.where(keep, out, 0.0).astype(o_ref.dtype)

        head_loop(group, 2, head)

    used = i * bq < new_count
    for n in range(chunks):
        mine = (hist_count > n * chunk) & (hist_count <= (n + 1) * chunk)
        pl.when(used & mine)(functools.partial(variant, n))

    @pl.when(jnp.logical_not(used))
    def _():
        o_ref[...] = jnp.zeros_like(o_ref)


def local(pool, table, hist_len, new_len, queries, new_kv):
    stores = lax.axis_size("store")
    tp = lax.axis_size("tp")
    store_index = lax.axis_index("store")
    slots_dev, piece, kv_all, _, hd = pool.shape[1:]
    block_len = piece * tp
    blocks_all = table.shape[2]
    sessions = table.shape[0]
    per_store = blocks_all // stores
    new_tokens, heads_dev = queries.shape[2:4]
    kv_dev = new_kv.shape[3]
    new_blocks = new_tokens // block_len
    hist_blocks = blocks_all - new_blocks
    hist_tokens = hist_blocks * block_len
    cap_new = min(per_store, new_blocks)
    group = heads_dev // kv_dev
    factor = math.log2(math.e) / math.sqrt(hd)
    bq = min(256, new_tokens)
    pair = 2 * hd
    own_hist = lax.dynamic_index_in_dim(hist_len, store_index, 0, keepdims=False)
    own_new = lax.dynamic_index_in_dim(new_len, store_index, 0, keepdims=False)
    local_ids = jnp.arange(slots_dev, dtype=jnp.int32)
    slot_base = store_index * slots_dev
    layer_table = table[:, 0, :]

    item_owner = jnp.repeat(jnp.arange(sessions, dtype=jnp.int32), blocks_all)
    matches = layer_table.reshape(-1)[:, None] == (slot_base + local_ids)[None, :]
    holder = jnp.sum(jnp.where(matches, item_owner[:, None], 0), axis=0)
    order_key = holder * slots_dev + local_ids
    rank = jnp.sum((order_key[None, :] < order_key[:, None]).astype(jnp.int32), axis=1)
    send_order = jnp.sum(jnp.where(rank[None, :] == local_ids[:, None], local_ids[None, :], 0), axis=1)
    outgoing = jnp.take(pool[0], send_order, axis=0)
    arrived = lax.all_to_all(outgoing, "store", split_axis=0, concat_axis=0, tiled=True)
    own_slots = lax.dynamic_index_in_dim(layer_table, store_index, 0, keepdims=False)
    arrive_rank = jnp.sum((own_slots[None, :] < own_slots[:, None]).astype(jnp.int32), axis=1)
    held = jnp.take(arrived, arrive_rank[:hist_blocks], axis=0)
    held = held.reshape(hist_blocks, piece, tp, kv_dev * pair).transpose(2, 0, 1, 3)
    history = lax.all_to_all(held, "tp", split_axis=0, concat_axis=0, tiled=True)

    q2d = queries.reshape(new_tokens, heads_dev * hd)
    kv2d = new_kv.reshape(new_tokens, kv_dev * pair)
    width = group * hd
    params = pltpu.CompilerParams(
        vmem_limit_bytes=VMEM_BYTES, dimension_semantics=("arbitrary", "arbitrary")
    )
    steps = new_tokens // bq
    smem = pl.BlockSpec(memory_space=pltpu.SMEM)
    q_spec = pl.BlockSpec((bq, width), lambda k, i: (i, k))
    lse_spec = pl.BlockSpec((1, bq, 128), lambda k, i: (k, i, 0))
    fresh_flops = 4 * new_tokens * new_tokens * heads_dev * hd
    part, lse = pl.pallas_call(
        functools.partial(fresh_kernel, group, hd, factor),
        grid=(kv_dev, steps),
        in_specs=[smem, q_spec, pl.BlockSpec((new_tokens, pair), lambda k, i: (0, k))],
        out_specs=[q_spec, lse_spec],
        out_shape=[
            jax.ShapeDtypeStruct((new_tokens, heads_dev * hd), jnp.float32),
            jax.ShapeDtypeStruct((kv_dev, new_tokens, 128), jnp.float32),
        ],
        scratch_shapes=[pltpu.VMEM((new_tokens, pair), jnp.bfloat16)] * 2,
        compiler_params=params,
        cost_estimate=pl.CostEstimate(
            flops=fresh_flops, bytes_accessed=6 * q2d.size, transcendentals=fresh_flops // 8 // hd
        ),
        name="attend_fresh",
    )(own_new.reshape(1), q2d, kv2d)

    hist_flops = 4 * new_tokens * hist_tokens * heads_dev * hd
    attended = pl.pallas_call(
        functools.partial(hist_kernel, group, hd, factor),
        grid=(kv_dev, steps),
        in_specs=[
            smem,
            q_spec,
            pl.BlockSpec((tp, hist_blocks, piece, pair), lambda k, i: (0, 0, 0, k)),
            q_spec,
            lse_spec,
        ],
        out_specs=q_spec,
        out_shape=jax.ShapeDtypeStruct((new_tokens, heads_dev * hd), jnp.bfloat16),
        scratch_shapes=[pltpu.VMEM((hist_tokens, pair), jnp.bfloat16)] * 2,
        compiler_params=params,
        cost_estimate=pl.CostEstimate(
            flops=hist_flops, bytes_accessed=8 * q2d.size, transcendentals=hist_flops // 4 // hd
        ),
        name="attend_history",
    )(jnp.stack([own_hist, own_new]), q2d, history, part, lse)

    token_ids = jnp.arange(new_tokens, dtype=jnp.int32)
    fresh = jnp.where((token_ids < own_new)[:, None], kv2d, jnp.zeros_like(kv2d))
    pieces = fresh.reshape(new_blocks, tp, piece, kv_dev * pair).transpose(1, 0, 2, 3)
    spread = lax.all_to_all(pieces, "tp", split_axis=0, concat_axis=0, tiled=True)
    new_slots = layer_table[:, hist_blocks:]
    new_target = new_slots // slots_dev
    same_place = (new_target[:, :, None] == new_target[:, None, :]) & (
        new_slots[:, None, :] < new_slots[:, :, None]
    )
    earlier = jnp.sum(same_place.astype(jnp.int32), axis=2)
    own_target = lax.dynamic_index_in_dim(new_target, store_index, 0, keepdims=False)
    own_earlier = lax.dynamic_index_in_dim(earlier, store_index, 0, keepdims=False)
    cells = jnp.arange(stores * cap_new, dtype=jnp.int32)
    takes = (own_target * cap_new + own_earlier)[None, :] == cells[:, None]
    source = jnp.sum(jnp.where(takes, jnp.arange(new_blocks, dtype=jnp.int32)[None, :], 0), axis=1)
    by_block = spread.transpose(1, 2, 0, 3).reshape((new_blocks,) + pool.shape[2:])
    parcel = jnp.take(by_block, source, axis=0)
    landed = lax.all_to_all(parcel, "store", split_axis=0, concat_axis=0, tiled=True)
    position = jnp.arange(sessions, dtype=jnp.int32)[:, None] * cap_new + earlier
    local_slot = new_slots - slot_base
    hits = (new_target == store_index)[:, :, None] & (
        local_slot[:, :, None] == local_ids[None, None, :]
    )
    has_new = jnp.any(hits, axis=(0, 1))
    source_row = jnp.sum(jnp.where(hits, position[:, :, None], 0), axis=(0, 1))
    new_pool = jnp.where(
        has_new[:, None, None, None, None], jnp.take(landed, source_row, axis=0), pool[0]
    )
    return attended.reshape(queries.shape), new_pool[None]


def solution(mesh):
    placed = (
        P(None, ("groups", "store"), "tp", None, None, None),
        P("groups", None, None),
        P("groups"),
        P("groups"),
        P(None, ("groups", "store"), None, "tp", None),
        P(None, ("groups", "store"), None, "tp", None, None),
    )
    return jax.shard_map(
        local,
        mesh=mesh,
        in_specs=placed,
        out_specs=(
            P(None, ("groups", "store"), None, "tp", None),
            P(None, ("groups", "store"), "tp", None, None, None),
        ),
        check_vma=False,
    )
```

```python
import functools
import math

import jax
import jax.numpy as jnp
from jax import lax
from jax.experimental import pallas as pl
from jax.experimental.pallas import tpu as pltpu
from jax.sharding import PartitionSpec as P

NT = (((1,), (1,)), ((), ()))
VMEM_BYTES = 48 * 1024 * 1024


def scaled_pair(q, factor):
    full = q.astype(jnp.float32) * factor
    high = full.astype(jnp.bfloat16)
    low = (full - high.astype(jnp.float32)).astype(jnp.bfloat16)
    return jnp.concatenate([high, low], axis=1)


def scores_of(q2, keys):
    return lax.dot_general(q2, keys, NT, preferred_element_type=jnp.float32)


def split_kv(kv, kd, vd, rows):
    hd = kv.shape[1] // 2
    kd[rows, :hd] = kv[:, :hd]
    kd[rows, hd:] = kv[:, :hd]
    vd[rows, :hd] = kv[:, hd:]
    vd[rows, hd:] = jnp.ones((kv.shape[0], hd), kv.dtype)


def head_loop(group, unroll, body):
    def step(n, carry):
        for u in range(unroll):
            body(n * unroll + u)
        return carry

    lax.fori_loop(0, group // unroll, step, 0)


def exchange_steps(axis, count, source, target, send, recv):
    me = lax.axis_index(axis)
    copies = []
    for d in range(1, count):
        to = lax.rem(me + d, count)
        copies.append(
            pltpu.make_async_remote_copy(
                src_ref=source(to),
                dst_ref=target(me),
                send_sem=send.at[d],
                recv_sem=recv.at[d],
                device_id={axis: to},
                device_id_type=pl.DeviceIdType.MESH,
            )
        )
    return copies


def fresh_kernel(
    group, hd, factor, stores, tp,
    order_ref, pick_ref, source_ref, q_ref, kv_ref, fresh_ref, pool_ref,
    o_ref, lse_ref, hist_ref, landed_ref,
    kd, vd, outbox, arrived, pieces, spread, parcel,
    send_a, recv_a, send_b, recv_b, send_c, recv_c, send_d, recv_d, own_sem,
):
    i = pl.program_id(1)
    turn = pl.program_id(0) * pl.num_programs(1) + i
    turns = pl.num_programs(0) * pl.num_programs(1)
    bq = q_ref.shape[0]
    steps = kd.shape[0] // bq
    s = lax.axis_index("store")
    z = lax.axis_index("tp")
    per = arrived.shape[0] // stores
    cap = parcel.shape[0] // stores
    blocks = pieces.shape[1]
    width = pieces.shape[3]

    hist_store = exchange_steps(
        "store", stores, lambda t: outbox.at[pl.ds(t * per, per)],
        lambda me: arrived.at[pl.ds(me * per, per)], send_a, recv_a,
    )
    new_tp = exchange_steps(
        "tp", tp, lambda t: fresh_ref.at[:, t], lambda me: spread.at[me], send_b, recv_b
    )
    hist_tp = exchange_steps(
        "tp", tp, lambda t: pieces.at[t], lambda me: hist_ref.at[me], send_c, recv_c
    )
    new_store = exchange_steps(
        "store", stores, lambda t: parcel.at[pl.ds(t * cap, cap)],
        lambda me: landed_ref.at[pl.ds(me * cap, cap)], send_d, recv_d,
    )
    own = [
        pltpu.make_async_copy(pieces.at[z], hist_ref.at[z], own_sem.at[0]),
        pltpu.make_async_copy(
            parcel.at[pl.ds(s * cap, cap)], landed_ref.at[pl.ds(s * cap, cap)], own_sem.at[1]
        ),
    ]

    @pl.when(turn == 0)
    def _():
        barrier = pltpu.get_barrier_semaphore()
        for axis, count in (("store", stores), ("tp", tp)):
            me = lax.axis_index(axis)
            for d in range(1, count):
                pl.semaphore_signal(
                    barrier, inc=1, device_id={axis: lax.rem(me + d, count)},
                    device_id_type=pl.DeviceIdType.MESH,
                )
        pl.semaphore_wait(barrier, stores + tp - 2)
        for copy in new_tp:
            copy.start()
        for d in range(1, stores):
            to = lax.rem(s + d, stores)

            def place(c, carry):
                outbox[to * per + c] = pool_ref[order_ref[to * per + c]]
                return carry

            lax.fori_loop(0, per, place, 0)
            hist_store[d - 1].start()

        def keep(c, carry):
            arrived[s * per + c] = pool_ref[order_ref[s * per + c]]
            return carry

        lax.fori_loop(0, per, keep, 0)
        spread[z] = fresh_ref[:, z]

    @pl.when(turn == turns // 2)
    def _():
        for copy in hist_store:
            copy.wait()

        def cut(b, carry):
            block = arrived[pick_ref[b]]
            for t in range(tp):
                pieces[t, b] = block[:, t * width : (t + 1) * width]
            return carry

        lax.fori_loop(0, blocks, cut, 0)
        for copy in hist_tp:
            copy.start()
        own[0].start()
        for copy in new_tp:
            copy.wait()

        def join(c, carry):
            n = source_ref[c]
            for t in range(tp):
                parcel[c, :, t * width : (t + 1) * width] = spread[t, n]
            return carry

        lax.fori_loop(0, stores * cap, join, 0)
        for copy in new_store:
            copy.start()
        own[1].start()

    @pl.when(i == 0)
    def _():
        split_kv(kv_ref[...], kd, vd, slice(None))

    def variant(n):
        lanes = lax.broadcasted_iota(jnp.int32, (bq, 128), 1)
        causal = lax.broadcasted_iota(jnp.int32, (bq, bq), 1) <= lax.broadcasted_iota(
            jnp.int32, (bq, bq), 0
        )

        def head(g):
            cols = pl.ds(pl.multiple_of(g * hd, hd), hd)
            q2 = scaled_pair(q_ref[:, cols], factor)
            edge = jnp.where(causal, scores_of(q2, kd[n * bq : (n + 1) * bq, :]), -jnp.inf)
            peak = jnp.max(edge, axis=1, keepdims=True)
            if n > 0:
                full = scores_of(q2, kd[: n * bq, :])
                peak = jnp.maximum(peak, jnp.max(full, axis=1, keepdims=True))
            p = jnp.exp2(edge - peak).astype(jnp.bfloat16)
            acc = jnp.dot(
                p, vd[n * bq : (n + 1) * bq, :], preferred_element_type=jnp.float32
            )
            if n > 0:
                p = jnp.exp2(full - peak).astype(jnp.bfloat16)
                acc += jnp.dot(p, vd[: n * bq, :], preferred_element_type=jnp.float32)
            total = acc[:, hd:]
            o_ref[:, cols] = acc[:, :hd] / total
            lse_ref[0] = jnp.where(lanes == g, peak + jnp.log2(total), lse_ref[0])

        lse_ref[0] = jnp.zeros_like(lse_ref[0])
        head_loop(group, 2, head)

    for n in range(steps):
        pl.when(i == n)(functools.partial(variant, n))

    @pl.when(turn == turns - 1)
    def _():
        for copy in hist_tp + new_store + own:
            copy.wait()


def hist_kernel(
    group, hd, factor, lens_ref, has_ref, row_ref, q_ref, kv_ref, of_ref, lse_ref, pool_ref,
    landed_ref, o_ref, out_pool_ref, kd, vd, save_sem,
):
    i = pl.program_id(1)
    turn = pl.program_id(0) * pl.num_programs(1) + i
    turns = pl.num_programs(0) * pl.num_programs(1)
    slots = pool_ref.shape[0]

    @pl.when(turn == 0)
    def _():
        for j in range(slots):
            new = has_ref[j] != 0

            @pl.when(new)
            def _():
                pltpu.make_async_copy(
                    landed_ref.at[row_ref[j]], out_pool_ref.at[j], save_sem.at[j]
                ).start()

            @pl.when(jnp.logical_not(new))
            def _():
                pltpu.make_async_copy(pool_ref.at[j], out_pool_ref.at[j], save_sem.at[j]).start()

    bq = q_ref.shape[0]
    chunk = min(256, kd.shape[0])
    chunks = kd.shape[0] // chunk
    hist_count = lens_ref[0]
    new_count = lens_ref[1]

    @pl.when(i == 0)
    def _():
        tp, blocks, piece, _ = kv_ref.shape
        for b in range(blocks):
            for z in range(tp):
                begin = (b * tp + z) * piece
                split_kv(kv_ref[z, b], kd, vd, slice(begin, begin + piece))

    def variant(n):
        lanes = lax.broadcasted_iota(jnp.int32, (bq, 128), 1)
        valid = lax.broadcasted_iota(jnp.int32, (bq, chunk), 1) < hist_count - n * chunk
        keep = lax.broadcasted_iota(jnp.int32, (bq, hd), 0) < new_count - i * bq

        def head(g):
            cols = pl.ds(pl.multiple_of(g * hd, hd), hd)
            q2 = scaled_pair(q_ref[:, cols], factor)
            lse = jnp.sum(jnp.where(lanes == g, lse_ref[0], 0.0), axis=1, keepdims=True)
            edge = jnp.where(valid, scores_of(q2, kd[n * chunk : (n + 1) * chunk, :]), -jnp.inf)
            peak = jnp.maximum(lse, jnp.max(edge, axis=1, keepdims=True))
            if n > 0:
                full = scores_of(q2, kd[: n * chunk, :])
                peak = jnp.maximum(peak, jnp.max(full, axis=1, keepdims=True))
            p = jnp.exp2(edge - peak).astype(jnp.bfloat16)
            acc = jnp.dot(
                p, vd[n * chunk : (n + 1) * chunk, :], preferred_element_type=jnp.float32
            )
            if n > 0:
                p = jnp.exp2(full - peak).astype(jnp.bfloat16)
                acc += jnp.dot(p, vd[: n * chunk, :], preferred_element_type=jnp.float32)
            share = jnp.exp2(lse - peak)
            out = (acc[:, :hd] + share * of_ref[:, cols]) / (acc[:, hd:] + share)
            o_ref[:, cols] = jnp.where(keep, out, 0.0).astype(o_ref.dtype)

        head_loop(group, 2, head)

    used = i * bq < new_count
    for n in range(chunks):
        mine = (hist_count > n * chunk) & (hist_count <= (n + 1) * chunk)
        pl.when(used & mine)(functools.partial(variant, n))

    @pl.when(jnp.logical_not(used))
    def _():
        o_ref[...] = jnp.zeros_like(o_ref)

    @pl.when(turn == turns - 1)
    def _():
        for j in range(slots):
            pltpu.make_async_copy(pool_ref.at[j], out_pool_ref.at[j], save_sem.at[j]).wait()


def local(pool, table, hist_len, new_len, queries, new_kv):
    stores = lax.axis_size("store")
    tp = lax.axis_size("tp")
    store_index = lax.axis_index("store")
    slots_dev, piece, kv_all, _, hd = pool.shape[1:]
    block_len = piece * tp
    blocks_all = table.shape[2]
    sessions = table.shape[0]
    per_store = blocks_all // stores
    new_tokens, heads_dev = queries.shape[2:4]
    kv_dev = new_kv.shape[3]
    new_blocks = new_tokens // block_len
    hist_blocks = blocks_all - new_blocks
    hist_tokens = hist_blocks * block_len
    cap_new = min(per_store, new_blocks)
    group = heads_dev // kv_dev
    factor = math.log2(math.e) / math.sqrt(hd)
    bq = min(256, new_tokens)
    pair = 2 * hd
    own_hist = lax.dynamic_index_in_dim(hist_len, store_index, 0, keepdims=False)
    own_new = lax.dynamic_index_in_dim(new_len, store_index, 0, keepdims=False)
    local_ids = jnp.arange(slots_dev, dtype=jnp.int32)
    slot_base = store_index * slots_dev
    layer_table = table[:, 0, :]

    rows = kv_all * pair
    width_kv = kv_dev * pair

    item_owner = jnp.repeat(jnp.arange(sessions, dtype=jnp.int32), blocks_all)
    matches = layer_table.reshape(-1)[:, None] == (slot_base + local_ids)[None, :]
    holder = jnp.sum(jnp.where(matches, item_owner[:, None], 0), axis=0)
    order_key = holder * slots_dev + local_ids
    rank = jnp.sum((order_key[None, :] < order_key[:, None]).astype(jnp.int32), axis=1)
    send_order = jnp.sum(jnp.where(rank[None, :] == local_ids[:, None], local_ids[None, :], 0), axis=1)
    own_slots = lax.dynamic_index_in_dim(layer_table, store_index, 0, keepdims=False)
    arrive_rank = jnp.sum((own_slots[None, :] < own_slots[:, None]).astype(jnp.int32), axis=1)
    new_slots = layer_table[:, hist_blocks:]
    new_target = new_slots // slots_dev
    same_place = (new_target[:, :, None] == new_target[:, None, :]) & (
        new_slots[:, None, :] < new_slots[:, :, None]
    )
    earlier = jnp.sum(same_place.astype(jnp.int32), axis=2)
    own_target = lax.dynamic_index_in_dim(new_target, store_index, 0, keepdims=False)
    own_earlier = lax.dynamic_index_in_dim(earlier, store_index, 0, keepdims=False)
    cells = jnp.arange(stores * cap_new, dtype=jnp.int32)
    takes = (own_target * cap_new + own_earlier)[None, :] == cells[:, None]
    source = jnp.sum(jnp.where(takes, jnp.arange(new_blocks, dtype=jnp.int32)[None, :], 0), axis=1)
    position = jnp.arange(sessions, dtype=jnp.int32)[:, None] * cap_new + earlier
    local_slot = new_slots - slot_base
    hits = (new_target == store_index)[:, :, None] & (
        local_slot[:, :, None] == local_ids[None, None, :]
    )
    has_new = jnp.any(hits, axis=(0, 1)).astype(jnp.int32)
    source_row = jnp.sum(jnp.where(hits, position[:, :, None], 0), axis=(0, 1))

    q2d = queries.reshape(new_tokens, heads_dev * hd)
    kv2d = new_kv.reshape(new_tokens, width_kv)
    token_ids = jnp.arange(new_tokens, dtype=jnp.int32)
    fresh = jnp.where((token_ids < own_new)[:, None], kv2d, jnp.zeros_like(kv2d))
    width = group * hd
    steps = new_tokens // bq
    smem = pl.BlockSpec(memory_space=pltpu.SMEM)
    vmem = pl.BlockSpec(memory_space=pltpu.VMEM)
    anywhere = pl.BlockSpec(memory_space=pl.ANY)
    q_spec = pl.BlockSpec((bq, width), lambda k, i: (i, k))
    lse_spec = pl.BlockSpec((1, bq, 128), lambda k, i: (k, i, 0))
    fresh_flops = 4 * new_tokens * new_tokens * heads_dev * hd
    bf16 = jnp.bfloat16
    part, lse, history, landed = pl.pallas_call(
        functools.partial(fresh_kernel, group, hd, factor, stores, tp),
        grid=(kv_dev, steps),
        in_specs=[
            smem, smem, smem, q_spec,
            pl.BlockSpec((new_tokens, pair), lambda k, i: (0, k)),
            vmem, vmem,
        ],
        out_specs=[q_spec, lse_spec, anywhere, anywhere],
        out_shape=[
            jax.ShapeDtypeStruct((new_tokens, heads_dev * hd), jnp.float32),
            jax.ShapeDtypeStruct((kv_dev, new_tokens, 128), jnp.float32),
            jax.ShapeDtypeStruct((tp, hist_blocks, piece, width_kv), bf16),
            jax.ShapeDtypeStruct((stores * cap_new, piece, rows), bf16),
        ],
        scratch_shapes=[
            pltpu.VMEM((new_tokens, pair), bf16),
            pltpu.VMEM((new_tokens, pair), bf16),
            pltpu.VMEM((slots_dev, piece, rows), bf16),
            pltpu.VMEM((blocks_all, piece, rows), bf16),
            pltpu.VMEM((tp, hist_blocks, piece, width_kv), bf16),
            pltpu.VMEM((tp, new_blocks, piece, width_kv), bf16),
            pltpu.VMEM((stores * cap_new, piece, rows), bf16),
            pltpu.SemaphoreType.DMA((stores,)),
            pltpu.SemaphoreType.DMA((stores,)),
            pltpu.SemaphoreType.DMA((tp,)),
            pltpu.SemaphoreType.DMA((tp,)),
            pltpu.SemaphoreType.DMA((tp,)),
            pltpu.SemaphoreType.DMA((tp,)),
            pltpu.SemaphoreType.DMA((stores,)),
            pltpu.SemaphoreType.DMA((stores,)),
            pltpu.SemaphoreType.DMA((2,)),
        ],
        compiler_params=pltpu.CompilerParams(
            vmem_limit_bytes=VMEM_BYTES,
            dimension_semantics=("arbitrary", "arbitrary"),
            collective_id=0,
            has_side_effects=True,
        ),
        cost_estimate=pl.CostEstimate(
            flops=fresh_flops, bytes_accessed=6 * q2d.size, transcendentals=fresh_flops // 8 // hd
        ),
        name="attend_fresh",
    )(
        send_order, arrive_rank[:hist_blocks], source, q2d, kv2d,
        fresh.reshape(new_blocks, tp, piece, width_kv), pool.reshape(slots_dev, piece, rows),
    )

    hist_flops = 4 * new_tokens * hist_tokens * heads_dev * hd
    slot_shape = (piece, kv_all * 2, hd)
    attended, new_pool = pl.pallas_call(
        functools.partial(hist_kernel, group, hd, factor),
        grid=(kv_dev, steps),
        in_specs=[
            smem, smem, smem, q_spec,
            pl.BlockSpec((tp, hist_blocks, piece, pair), lambda k, i: (0, 0, 0, k)),
            q_spec, lse_spec, anywhere, anywhere,
        ],
        out_specs=[q_spec, anywhere],
        out_shape=[
            jax.ShapeDtypeStruct((new_tokens, heads_dev * hd), bf16),
            jax.ShapeDtypeStruct((slots_dev,) + slot_shape, bf16),
        ],
        scratch_shapes=[
            pltpu.VMEM((hist_tokens, pair), bf16),
            pltpu.VMEM((hist_tokens, pair), bf16),
            pltpu.SemaphoreType.DMA((slots_dev,)),
        ],
        compiler_params=pltpu.CompilerParams(
            vmem_limit_bytes=VMEM_BYTES, dimension_semantics=("arbitrary", "arbitrary")
        ),
        cost_estimate=pl.CostEstimate(
            flops=hist_flops, bytes_accessed=8 * q2d.size, transcendentals=hist_flops // 4 // hd
        ),
        name="attend_history",
    )(
        jnp.stack([own_hist, own_new]), has_new, source_row, q2d, history, part, lse,
        pool.reshape((slots_dev,) + slot_shape), landed.reshape((-1,) + slot_shape),
    )
    return attended.reshape(queries.shape), new_pool.reshape(pool.shape)


def solution(mesh):
    placed = (
        P(None, ("groups", "store"), "tp", None, None, None),
        P("groups", None, None),
        P("groups"),
        P("groups"),
        P(None, ("groups", "store"), None, "tp", None),
        P(None, ("groups", "store"), None, "tp", None, None),
    )
    return jax.shard_map(
        local,
        mesh=mesh,
        in_specs=placed,
        out_specs=(
            P(None, ("groups", "store"), None, "tp", None),
            P(None, ("groups", "store"), "tp", None, None, None),
        ),
        check_vma=False,
    )
```

```python
import functools
import math

import jax
import jax.numpy as jnp
from jax import lax
from jax.experimental import pallas as pl
from jax.experimental.pallas import tpu as pltpu
from jax.sharding import PartitionSpec as P

NT = (((1,), (1,)), ((), ()))
VMEM_BYTES = 48 * 1024 * 1024


def scaled_pair(q, factor):
    full = q.astype(jnp.float32) * factor
    high = full.astype(jnp.bfloat16)
    low = (full - high.astype(jnp.float32)).astype(jnp.bfloat16)
    return jnp.concatenate([high, low], axis=1)


def scores_of(q2, keys):
    return lax.dot_general(q2, keys, NT, preferred_element_type=jnp.float32)


def split_kv(kv, kd, vd, rows):
    hd = kv.shape[1] // 2
    kd[rows, :hd] = kv[:, :hd]
    kd[rows, hd:] = kv[:, :hd]
    vd[rows, :hd] = kv[:, hd:]
    vd[rows, hd:] = jnp.ones((kv.shape[0], hd), kv.dtype)


def head_loop(group, unroll, body):
    def step(n, carry):
        for u in range(unroll):
            body(n * unroll + u)
        return carry

    lax.fori_loop(0, group // unroll, step, 0)


def exchange_steps(axis, count, source, target, send, recv):
    me = lax.axis_index(axis)
    copies = []
    for d in range(1, count):
        to = lax.rem(me + d, count)
        copies.append(
            pltpu.make_async_remote_copy(
                src_ref=source(to),
                dst_ref=target(me),
                send_sem=send.at[d],
                recv_sem=recv.at[d],
                device_id={axis: to},
                device_id_type=pl.DeviceIdType.MESH,
            )
        )
    return copies


def fresh_kernel(
    group, hd, factor, stores, tp,
    order_ref, pick_ref, source_ref, q_ref, kv_ref, fresh_ref, pool_ref,
    o_ref, lse_ref, hist_ref, landed_ref,
    kd, vd, outbox, arrived, pieces, spread, parcel,
    send_a, recv_a, send_b, recv_b, send_c, recv_c, send_d, recv_d, own_sem,
):
    i = pl.program_id(1)
    turn = pl.program_id(0) * pl.num_programs(1) + i
    turns = pl.num_programs(0) * pl.num_programs(1)
    bq = q_ref.shape[0]
    steps = kd.shape[0] // bq
    s = lax.axis_index("store")
    z = lax.axis_index("tp")
    per = arrived.shape[0] // stores
    cap = parcel.shape[0] // stores
    blocks = pieces.shape[1]
    width = pieces.shape[3]

    hist_store = exchange_steps(
        "store", stores, lambda t: outbox.at[pl.ds(t * per, per)],
        lambda me: arrived.at[pl.ds(me * per, per)], send_a, recv_a,
    )
    new_tp = exchange_steps(
        "tp", tp, lambda t: fresh_ref.at[:, t], lambda me: spread.at[me], send_b, recv_b
    )
    hist_tp = exchange_steps(
        "tp", tp, lambda t: pieces.at[t], lambda me: hist_ref.at[me], send_c, recv_c
    )
    new_store = exchange_steps(
        "store", stores, lambda t: parcel.at[pl.ds(t * cap, cap)],
        lambda me: landed_ref.at[pl.ds(me * cap, cap)], send_d, recv_d,
    )
    own = [
        pltpu.make_async_copy(pieces.at[z], hist_ref.at[z], own_sem.at[0]),
        pltpu.make_async_copy(
            parcel.at[pl.ds(s * cap, cap)], landed_ref.at[pl.ds(s * cap, cap)], own_sem.at[1]
        ),
    ]

    @pl.when(turn == 0)
    def _():
        barrier = pltpu.get_barrier_semaphore()
        for axis, count in (("store", stores), ("tp", tp)):
            me = lax.axis_index(axis)
            for d in range(1, count):
                pl.semaphore_signal(
                    barrier, inc=1, device_id={axis: lax.rem(me + d, count)},
                    device_id_type=pl.DeviceIdType.MESH,
                )
        pl.semaphore_wait(barrier, stores + tp - 2)
        for copy in new_tp:
            copy.start()
        for d in range(1, stores):
            to = lax.rem(s + d, stores)

            def place(c, carry):
                outbox[to * per + c] = pool_ref[order_ref[to * per + c]]
                return carry

            lax.fori_loop(0, per, place, 0)
            hist_store[d - 1].start()

        def keep(c, carry):
            arrived[s * per + c] = pool_ref[order_ref[s * per + c]]
            return carry

        lax.fori_loop(0, per, keep, 0)
        spread[z] = fresh_ref[:, z]

    @pl.when(turn == turns // 2)
    def _():
        for copy in hist_store:
            copy.wait()

        def cut(b, carry):
            block = arrived[pick_ref[b]]
            for t in range(tp):
                pieces[t, b] = block[:, t * width : (t + 1) * width]
            return carry

        lax.fori_loop(0, blocks, cut, 0)
        for copy in hist_tp:
            copy.start()
        own[0].start()
        for copy in new_tp:
            copy.wait()

        def join(c, carry):
            n = source_ref[c]
            for t in range(tp):
                parcel[c, :, t * width : (t + 1) * width] = spread[t, n]
            return carry

        lax.fori_loop(0, stores * cap, join, 0)
        for copy in new_store:
            copy.start()
        own[1].start()

    @pl.when(i == 0)
    def _():
        split_kv(kv_ref[...], kd, vd, slice(None))

    def variant(n):
        lanes = lax.broadcasted_iota(jnp.int32, (bq, 128), 1)
        causal = lax.broadcasted_iota(jnp.int32, (bq, bq), 1) <= lax.broadcasted_iota(
            jnp.int32, (bq, bq), 0
        )

        def head(g):
            cols = pl.ds(pl.multiple_of(g * hd, hd), hd)
            q2 = scaled_pair(q_ref[:, cols], factor)
            edge = jnp.where(causal, scores_of(q2, kd[n * bq : (n + 1) * bq, :]), -jnp.inf)
            peak = jnp.max(edge, axis=1, keepdims=True)
            if n > 0:
                full = scores_of(q2, kd[: n * bq, :])
                peak = jnp.maximum(peak, jnp.max(full, axis=1, keepdims=True))
            p = jnp.exp2(edge - peak).astype(jnp.bfloat16)
            acc = jnp.dot(
                p, vd[n * bq : (n + 1) * bq, :], preferred_element_type=jnp.float32
            )
            if n > 0:
                p = jnp.exp2(full - peak).astype(jnp.bfloat16)
                acc += jnp.dot(p, vd[: n * bq, :], preferred_element_type=jnp.float32)
            total = acc[:, hd:]
            o_ref[:, cols] = acc[:, :hd] / total
            lse_ref[0] = jnp.where(lanes == g, peak + jnp.log2(total), lse_ref[0])

        lse_ref[0] = jnp.zeros_like(lse_ref[0])
        head_loop(group, math.gcd(group, 6), head)

    for n in range(steps):
        pl.when(i == n)(functools.partial(variant, n))

    @pl.when(turn == turns - 1)
    def _():
        for copy in hist_tp + new_store + own:
            copy.wait()


def hist_kernel(
    group, hd, factor, lens_ref, has_ref, row_ref, q_ref, kv_ref, of_ref, lse_ref, pool_ref,
    landed_ref, o_ref, out_pool_ref, kd, vd, save_sem,
):
    i = pl.program_id(1)
    turn = pl.program_id(0) * pl.num_programs(1) + i
    turns = pl.num_programs(0) * pl.num_programs(1)
    slots = pool_ref.shape[0]

    @pl.when(turn == 0)
    def _():
        for j in range(slots):
            new = has_ref[j] != 0

            @pl.when(new)
            def _():
                pltpu.make_async_copy(
                    landed_ref.at[row_ref[j]], out_pool_ref.at[j], save_sem.at[j]
                ).start()

            @pl.when(jnp.logical_not(new))
            def _():
                pltpu.make_async_copy(pool_ref.at[j], out_pool_ref.at[j], save_sem.at[j]).start()

    bq = q_ref.shape[0]
    chunk = min(256, kd.shape[0])
    chunks = kd.shape[0] // chunk
    hist_count = lens_ref[0]
    new_count = lens_ref[1]

    @pl.when(i == 0)
    def _():
        tp, blocks, piece, _ = kv_ref.shape
        for b in range(blocks):
            for z in range(tp):
                begin = (b * tp + z) * piece
                split_kv(kv_ref[z, b], kd, vd, slice(begin, begin + piece))

    def variant(n):
        lanes = lax.broadcasted_iota(jnp.int32, (bq, 128), 1)
        valid = lax.broadcasted_iota(jnp.int32, (bq, chunk), 1) < hist_count - n * chunk
        keep = lax.broadcasted_iota(jnp.int32, (bq, hd), 0) < new_count - i * bq

        def head(g):
            cols = pl.ds(pl.multiple_of(g * hd, hd), hd)
            q2 = scaled_pair(q_ref[:, cols], factor)
            lse = jnp.sum(jnp.where(lanes == g, lse_ref[0], 0.0), axis=1, keepdims=True)
            edge = jnp.where(valid, scores_of(q2, kd[n * chunk : (n + 1) * chunk, :]), -jnp.inf)
            peak = jnp.maximum(lse, jnp.max(edge, axis=1, keepdims=True))
            if n > 0:
                full = scores_of(q2, kd[: n * chunk, :])
                peak = jnp.maximum(peak, jnp.max(full, axis=1, keepdims=True))
            p = jnp.exp2(edge - peak).astype(jnp.bfloat16)
            acc = jnp.dot(
                p, vd[n * chunk : (n + 1) * chunk, :], preferred_element_type=jnp.float32
            )
            if n > 0:
                p = jnp.exp2(full - peak).astype(jnp.bfloat16)
                acc += jnp.dot(p, vd[: n * chunk, :], preferred_element_type=jnp.float32)
            share = jnp.exp2(lse - peak)
            out = (acc[:, :hd] + share * of_ref[:, cols]) / (acc[:, hd:] + share)
            o_ref[:, cols] = jnp.where(keep, out, 0.0).astype(o_ref.dtype)

        head_loop(group, math.gcd(group, 6), head)

    used = i * bq < new_count
    for n in range(chunks):
        mine = (hist_count > n * chunk) & (hist_count <= (n + 1) * chunk)
        pl.when(used & mine)(functools.partial(variant, n))

    @pl.when(jnp.logical_not(used))
    def _():
        o_ref[...] = jnp.zeros_like(o_ref)

    @pl.when(turn == turns - 1)
    def _():
        for j in range(slots):
            pltpu.make_async_copy(pool_ref.at[j], out_pool_ref.at[j], save_sem.at[j]).wait()


def local(pool, table, hist_len, new_len, queries, new_kv):
    stores = lax.axis_size("store")
    tp = lax.axis_size("tp")
    store_index = lax.axis_index("store")
    slots_dev, piece, kv_all, _, hd = pool.shape[1:]
    block_len = piece * tp
    blocks_all = table.shape[2]
    sessions = table.shape[0]
    per_store = blocks_all // stores
    new_tokens, heads_dev = queries.shape[2:4]
    kv_dev = new_kv.shape[3]
    new_blocks = new_tokens // block_len
    hist_blocks = blocks_all - new_blocks
    hist_tokens = hist_blocks * block_len
    cap_new = min(per_store, new_blocks)
    group = heads_dev // kv_dev
    factor = math.log2(math.e) / math.sqrt(hd)
    bq = min(256, new_tokens)
    pair = 2 * hd
    own_hist = lax.dynamic_index_in_dim(hist_len, store_index, 0, keepdims=False)
    own_new = lax.dynamic_index_in_dim(new_len, store_index, 0, keepdims=False)
    local_ids = jnp.arange(slots_dev, dtype=jnp.int32)
    slot_base = store_index * slots_dev
    layer_table = table[:, 0, :]

    rows = kv_all * pair
    width_kv = kv_dev * pair

    item_owner = jnp.repeat(jnp.arange(sessions, dtype=jnp.int32), blocks_all)
    matches = layer_table.reshape(-1)[:, None] == (slot_base + local_ids)[None, :]
    holder = jnp.sum(jnp.where(matches, item_owner[:, None], 0), axis=0)
    order_key = holder * slots_dev + local_ids
    rank = jnp.sum((order_key[None, :] < order_key[:, None]).astype(jnp.int32), axis=1)
    send_order = jnp.sum(jnp.where(rank[None, :] == local_ids[:, None], local_ids[None, :], 0), axis=1)
    own_slots = lax.dynamic_index_in_dim(layer_table, store_index, 0, keepdims=False)
    arrive_rank = jnp.sum((own_slots[None, :] < own_slots[:, None]).astype(jnp.int32), axis=1)
    new_slots = layer_table[:, hist_blocks:]
    new_target = new_slots // slots_dev
    same_place = (new_target[:, :, None] == new_target[:, None, :]) & (
        new_slots[:, None, :] < new_slots[:, :, None]
    )
    earlier = jnp.sum(same_place.astype(jnp.int32), axis=2)
    own_target = lax.dynamic_index_in_dim(new_target, store_index, 0, keepdims=False)
    own_earlier = lax.dynamic_index_in_dim(earlier, store_index, 0, keepdims=False)
    cells = jnp.arange(stores * cap_new, dtype=jnp.int32)
    takes = (own_target * cap_new + own_earlier)[None, :] == cells[:, None]
    source = jnp.sum(jnp.where(takes, jnp.arange(new_blocks, dtype=jnp.int32)[None, :], 0), axis=1)
    position = jnp.arange(sessions, dtype=jnp.int32)[:, None] * cap_new + earlier
    local_slot = new_slots - slot_base
    hits = (new_target == store_index)[:, :, None] & (
        local_slot[:, :, None] == local_ids[None, None, :]
    )
    has_new = jnp.any(hits, axis=(0, 1)).astype(jnp.int32)
    source_row = jnp.sum(jnp.where(hits, position[:, :, None], 0), axis=(0, 1))

    q2d = queries.reshape(new_tokens, heads_dev * hd)
    kv2d = new_kv.reshape(new_tokens, width_kv)
    token_ids = jnp.arange(new_tokens, dtype=jnp.int32)
    fresh = jnp.where((token_ids < own_new)[:, None], kv2d, jnp.zeros_like(kv2d))
    width = group * hd
    steps = new_tokens // bq
    smem = pl.BlockSpec(memory_space=pltpu.SMEM)
    vmem = pl.BlockSpec(memory_space=pltpu.VMEM)
    anywhere = pl.BlockSpec(memory_space=pl.ANY)
    q_spec = pl.BlockSpec((bq, width), lambda k, i: (i, k))
    lse_spec = pl.BlockSpec((1, bq, 128), lambda k, i: (k, i, 0))
    fresh_flops = 4 * new_tokens * new_tokens * heads_dev * hd
    bf16 = jnp.bfloat16
    part, lse, history, landed = pl.pallas_call(
        functools.partial(fresh_kernel, group, hd, factor, stores, tp),
        grid=(kv_dev, steps),
        in_specs=[
            smem, smem, smem, q_spec,
            pl.BlockSpec((new_tokens, pair), lambda k, i: (0, k)),
            vmem, vmem,
        ],
        out_specs=[q_spec, lse_spec, anywhere, anywhere],
        out_shape=[
            jax.ShapeDtypeStruct((new_tokens, heads_dev * hd), jnp.float32),
            jax.ShapeDtypeStruct((kv_dev, new_tokens, 128), jnp.float32),
            jax.ShapeDtypeStruct((tp, hist_blocks, piece, width_kv), bf16),
            jax.ShapeDtypeStruct((stores * cap_new, piece, rows), bf16),
        ],
        scratch_shapes=[
            pltpu.VMEM((new_tokens, pair), bf16),
            pltpu.VMEM((new_tokens, pair), bf16),
            pltpu.VMEM((slots_dev, piece, rows), bf16),
            pltpu.VMEM((blocks_all, piece, rows), bf16),
            pltpu.VMEM((tp, hist_blocks, piece, width_kv), bf16),
            pltpu.VMEM((tp, new_blocks, piece, width_kv), bf16),
            pltpu.VMEM((stores * cap_new, piece, rows), bf16),
            pltpu.SemaphoreType.DMA((stores,)),
            pltpu.SemaphoreType.DMA((stores,)),
            pltpu.SemaphoreType.DMA((tp,)),
            pltpu.SemaphoreType.DMA((tp,)),
            pltpu.SemaphoreType.DMA((tp,)),
            pltpu.SemaphoreType.DMA((tp,)),
            pltpu.SemaphoreType.DMA((stores,)),
            pltpu.SemaphoreType.DMA((stores,)),
            pltpu.SemaphoreType.DMA((2,)),
        ],
        compiler_params=pltpu.CompilerParams(
            vmem_limit_bytes=VMEM_BYTES,
            dimension_semantics=("arbitrary", "arbitrary"),
            collective_id=0,
            has_side_effects=True,
        ),
        cost_estimate=pl.CostEstimate(
            flops=fresh_flops, bytes_accessed=6 * q2d.size, transcendentals=fresh_flops // 8 // hd
        ),
        name="attend_fresh",
    )(
        send_order, arrive_rank[:hist_blocks], source, q2d, kv2d,
        fresh.reshape(new_blocks, tp, piece, width_kv), pool.reshape(slots_dev, piece, rows),
    )

    hist_flops = 4 * new_tokens * hist_tokens * heads_dev * hd
    slot_shape = (piece, kv_all * 2, hd)
    attended, new_pool = pl.pallas_call(
        functools.partial(hist_kernel, group, hd, factor),
        grid=(kv_dev, steps),
        in_specs=[
            smem, smem, smem, q_spec,
            pl.BlockSpec((tp, hist_blocks, piece, pair), lambda k, i: (0, 0, 0, k)),
            q_spec, lse_spec, anywhere, anywhere,
        ],
        out_specs=[q_spec, anywhere],
        out_shape=[
            jax.ShapeDtypeStruct((new_tokens, heads_dev * hd), bf16),
            jax.ShapeDtypeStruct((slots_dev,) + slot_shape, bf16),
        ],
        scratch_shapes=[
            pltpu.VMEM((hist_tokens, pair), bf16),
            pltpu.VMEM((hist_tokens, pair), bf16),
            pltpu.SemaphoreType.DMA((slots_dev,)),
        ],
        compiler_params=pltpu.CompilerParams(
            vmem_limit_bytes=VMEM_BYTES, dimension_semantics=("arbitrary", "arbitrary")
        ),
        cost_estimate=pl.CostEstimate(
            flops=hist_flops, bytes_accessed=8 * q2d.size, transcendentals=hist_flops // 4 // hd
        ),
        name="attend_history",
    )(
        jnp.stack([own_hist, own_new]), has_new, source_row, q2d, history, part, lse,
        pool.reshape((slots_dev,) + slot_shape), landed.reshape((-1,) + slot_shape),
    )
    return attended.reshape(queries.shape), new_pool.reshape(pool.shape)


def solution(mesh):
    placed = (
        P(None, ("groups", "store"), "tp", None, None, None),
        P("groups", None, None),
        P("groups"),
        P("groups"),
        P(None, ("groups", "store"), None, "tp", None),
        P(None, ("groups", "store"), None, "tp", None, None),
    )
    return jax.shard_map(
        local,
        mesh=mesh,
        in_specs=placed,
        out_specs=(
            P(None, ("groups", "store"), None, "tp", None),
            P(None, ("groups", "store"), "tp", None, None, None),
        ),
        check_vma=False,
    )
```
